32 devices in a mesh: dp: 8 (over z, x), tensor: 4 (over y, core).
Axes of the slice: x: 2, y: 2, z: 4, core: 2. Of those that a mesh axis runs over, the one named last changes fastest.
Arguments:
- tokens: bfloat16 [4096, 768], P('dp'), may hold values from -6 to 6
- cotangent: bfloat16 [4096, 768], P('dp'), may hold values from -6 to 6
- seq_lengths: int32 [8, 1], P('dp'), may hold values from 192 to 512, as said below
- ln1_gain: float32 [768], replicated, may hold values from 0.5 to 1.5
- ln1_bias: float32 [768], replicated, may hold values from -1 to 1
- qkv_weight: bfloat16 [3, 768, 768], P(None, None, 'tensor'), may hold values from -0.21875 to 0.21875
- qv_bias: float32 [2, 768], P(None, 'tensor'), may hold values from -1.5 to 1.5
- out_weight: bfloat16 [768, 768], P('tensor'), may hold values from -1.75 to 1.75
- out_bias: float32 [768], replicated, may hold values from -1 to 1
- ln2_gain: float32 [768], replicated, may hold values from 0.5 to 1.5
- ln2_bias: float32 [768], replicated, may hold values from -1 to 1
- fc1_weight: bfloat16 [768, 3072], P(None, 'tensor'), may hold values from -0.21875 to 0.21875
- fc1_bias: float32 [3072], P('tensor'), may hold values from -1.5 to 1.5
- fc2_weight: bfloat16 [3072, 768], P('tensor'), may hold values from -0.109375 to 0.109375
- fc2_bias: float32 [768], replicated, may hold values from -1 to 1
Outputs:
- block_out: bfloat16 [4096, 768], P(('dp', 'tensor'))
- tokens_grad: float32 [4096, 768], P(('dp', 'tensor'))
- qkv_weight_grad: float32 [3, 768, 768], P(None, 'dp', 'tensor')
- qv_bias_grad: float32 [2, 768], P(None, 'tensor')
- out_weight_grad: float32 [768, 768], P('tensor', 'dp')
- out_bias_grad: float32 [768], replicated
- fc1_weight_grad: float32 [768, 3072], P('dp', 'tensor')
- fc1_bias_grad: float32 [3072], P('tensor')
- fc2_weight_grad: float32 [3072, 768], P('tensor', 'dp')
- fc2_bias_grad: float32 [768], replicated
- ln1_gain_grad: float32 [768], replicated
- ln1_bias_grad: float32 [768], replicated
- ln2_gain_grad: float32 [768], replicated
- ln2_bias_grad: float32 [768], replicated
The draws below stay inside these ranges and needn't reach their ends.
Inputs may be any that keep to these rules, and one draw needn't show every extreme that they name: `seq_lengths`: row d lists the lengths of the sequences that index d of dp holds, in order, nonzero ones first and zeros after; each index holds at least one sequence; each sequence starts at the first multiple of 128 rows after the end of the one before it, the first at the index's first row.
All inputs are finite; a program needn't handle non-finite values.
Results may differ from the reference program's by a relative error of at most 0.014.
Values may be sent and summed in bfloat16 or wider, within the bound.
A program may use at most 64 MiB of HBM per device.

```python
import jax
import jax.numpy as jnp
from jax import lax

D = 768
HEADS = 12
HEAD_DIM = 64
FF = 3072
MAXLEN = 512
PAD = 128
SLOTS = 1
CAP = 512
TOKENS = 4096
N_DP = 8


def draw_seq_lengths(key, part):
    key = jax.random.fold_in(key, 11)
    several = jax.random.split(key, 4)
    lengths = jax.random.randint(several[0], (N_DP, SLOTS), MAXLEN * 3 // 8, MAXLEN + 1)
    fewest = (SLOTS + 1) // 2
    live_count = jax.random.randint(several[1], (N_DP, 1), fewest, SLOTS + 1)
    short_dev = jax.random.randint(several[2], (), 0, N_DP)
    long_dev = (short_dev + 1 + jax.random.randint(several[3], (), 0, max(N_DP - 1, 1))) % N_DP
    device_ids = jnp.arange(N_DP)[:, None]
    slot_ids = jnp.arange(SLOTS)[None, :]
    live_count = jnp.where(device_ids == short_dev, fewest, live_count)
    lengths = jnp.where((device_ids == short_dev) & (slot_ids == fewest - 1), MAXLEN * 3 // 8, lengths)
    lengths = jnp.where((device_ids == long_dev) & (slot_ids == 0), MAXLEN, lengths)
    return jnp.where(slot_ids < live_count, lengths, 0).astype(jnp.int32)


def level_of(stream_key, shape, cuts, low, high):
    level, own = 1.0, jax.random.fold_in(stream_key, 6)
    for dim, blocks in cuts:
        steps = jnp.exp(jax.random.uniform(jax.random.fold_in(own, dim), (blocks,), jnp.float32, low / len(cuts), high / len(cuts)))
        level = level * jnp.repeat(steps, shape[dim] // blocks).reshape([-1 if axis == dim else 1 for axis in range(len(shape))])
    return level


def centred(key, dims, scale, most, shards=(), kind=jnp.bfloat16):
    values = jax.random.normal(key, dims, jnp.float32) * scale
    if len(shards) > 0:
        values = level_of(key, dims, shards, -0.22, 0.18) * values
    return jnp.clip(values, min=-most, max=most).astype(kind)


def setup_inputs(seed: int = 0) -> dict:
    key_list = jax.random.split(jax.random.key(seed), 16)
    tokens = centred(key_list[0], (TOKENS, D), 1.0, 6.0, ((0, 8),))
    cotangent = centred(key_list[1], (TOKENS, D), 1.0, 6.0, ((0, 8),))
    seq_lengths = draw_seq_lengths(jax.random.fold_in(key_list[15], 71), 0)
    ln1_gain = jnp.clip(1.0 + 0.1 * jax.random.normal(key_list[3], (D,), jnp.float32), 0.5, 1.5)
    ln1_bias = centred(key_list[4], (D,), 0.2, 1.0, (), jnp.float32)
    qkv_weight = centred(key_list[5], (3, D, D), D ** -0.5, 0.21875, ((2, 4),))
    qv_bias = centred(key_list[6], (2, D), 0.3, 1.5, ((1, 4),), jnp.float32)
    out_weight = centred(key_list[7], (D, D), 12 ** -0.5, 1.75, ((0, 4),))
    out_bias = centred(key_list[8], (D,), 0.2, 1.0, (), jnp.float32)
    ln2_gain = jnp.clip(1.0 + 0.1 * jax.random.normal(key_list[9], (D,), jnp.float32), 0.5, 1.5)
    ln2_bias = centred(key_list[10], (D,), 0.2, 1.0, (), jnp.float32)
    fc1_weight = centred(key_list[11], (D, FF), D ** -0.5, 0.21875, ((1, 4),))
    fc1_bias = centred(key_list[12], (FF,), 0.3, 1.5, ((0, 4),), jnp.float32)
    fc2_weight = centred(key_list[13], (FF, D), FF ** -0.5, 0.109375, ((0, 4),))
    fc2_bias = centred(key_list[14], (D,), 0.2, 1.0, (), jnp.float32)
    return {"tokens": tokens, "cotangent": cotangent, "seq_lengths": seq_lengths, "ln1_gain": ln1_gain, "ln1_bias": ln1_bias, "qkv_weight": qkv_weight, "qv_bias": qv_bias, "out_weight": out_weight, "out_bias": out_bias, "ln2_gain": ln2_gain, "ln2_bias": ln2_bias, "fc1_weight": fc1_weight, "fc1_bias": fc1_bias, "fc2_weight": fc2_weight, "fc2_bias": fc2_bias}


EPS = 1e-05
NEG = -1e+30
HIGH = lax.Precision.HIGHEST

@jax.custom_vjp
def low(v):
    return lax.optimization_barrier(v.astype(jnp.bfloat16)).astype(jnp.float32)

@jax.custom_vjp
def low_back(v):
    return v

def low_keep(v):
    return (low(v), None)

def low_pass(kept, grad):
    return (grad,)

def back_keep(v):
    return (v, None)

def back_low(kept, grad):
    return (low(grad),)
low.defvjp(low_keep, low_pass)
low_back.defvjp(back_keep, back_low)

def layer_norm(values, gain, shift):
    center = values - lax.optimization_barrier(jnp.mean(values, axis=-1, keepdims=True))
    spread = lax.optimization_barrier(jnp.mean(center * center, axis=-1, keepdims=True))
    return center * lax.rsqrt(spread + EPS) * gain + shift

def layout(lengths, row_count):
    padded = (lengths + PAD - 1) // PAD * PAD
    starts = (jnp.cumsum(padded) - padded).astype(jnp.int32)
    position = jnp.arange(row_count, dtype=jnp.int32)[:, None]
    inside = (position >= starts[None, :]) & (position < (starts + lengths)[None, :])
    slot_ids = jnp.arange(lengths.shape[0], dtype=jnp.int32)[None, :]
    valid = jnp.any(inside, axis=1)
    chosen = lax.optimization_barrier(jnp.sum(jnp.where(inside, slot_ids, 0), axis=1)).astype(jnp.int32)
    return (valid, jnp.where(valid, chosen, -1).astype(jnp.int32))

def window_mask(start_row, segment, seg_pad, valid_pad, reach):
    q_pos = start_row + jnp.arange(MAXLEN, dtype=jnp.int32)
    k_pos = start_row - reach + jnp.arange(MAXLEN + reach, dtype=jnp.int32)
    q_seg = lax.dynamic_slice_in_dim(segment, start_row, MAXLEN)
    k_seg = lax.dynamic_slice_in_dim(seg_pad, start_row, MAXLEN + reach)
    k_valid = lax.dynamic_slice_in_dim(valid_pad, start_row, MAXLEN + reach)
    same = k_valid[None, :] & (q_seg[:, None] == k_seg[None, :]) & (k_pos[None, :] <= q_pos[:, None])
    return same | (k_pos[None, :] == q_pos[:, None])

def attend_block(q_block, k_window, v_window, allowed):
    scores = jnp.einsum('qhd,khd->hqk', q_block, k_window, precision=HIGH) * HEAD_DIM ** (-0.5)
    scores = jnp.where(allowed[None], low_back(scores), NEG)
    row_max = lax.optimization_barrier(jnp.max(scores, axis=-1, keepdims=True))
    weights = jnp.exp(scores - row_max)
    prob = weights / lax.optimization_barrier(jnp.sum(weights, axis=-1, keepdims=True))
    return jnp.einsum('hqk,khd->qhd', low(prob), v_window, precision=HIGH)

def forward(tokens_f, valid, segment, params):
    ln1_gain, ln1_bias, qkv_weight, qv_bias, out_weight, out_bias, ln2_gain, ln2_bias, fc1_weight, fc1_bias, fc2_weight, fc2_bias = params
    reach = min(MAXLEN - PAD, CAP - MAXLEN)
    normed = low(layer_norm(tokens_f, ln1_gain, ln1_bias))
    project = jnp.einsum('td,jde->jte', normed, qkv_weight, precision=HIGH)
    query = low_back(low(project[0] + qv_bias[0])).reshape(CAP, HEADS, HEAD_DIM)
    keys_all = low_back(low(project[1])).reshape(CAP, HEADS, HEAD_DIM)
    values_all = low_back(low(project[2] + qv_bias[1])).reshape(CAP, HEADS, HEAD_DIM)
    blank = jnp.zeros((reach, HEADS, HEAD_DIM), jnp.float32)
    key_pad = jnp.concatenate([blank, keys_all], axis=0)
    value_pad = jnp.concatenate([blank, values_all], axis=0)
    seg_pad = jnp.concatenate([jnp.full((reach,), -1, jnp.int32), segment])
    valid_pad = jnp.concatenate([jnp.zeros((reach,), dtype=jnp.bool_), valid])

    def one_block(block_index):
        start_row = block_index * MAXLEN
        q_block = lax.dynamic_slice_in_dim(query, start_row, MAXLEN, 0)
        k_window = lax.dynamic_slice_in_dim(key_pad, start_row, MAXLEN + reach, 0)
        v_window = lax.dynamic_slice_in_dim(value_pad, start_row, MAXLEN + reach, 0)
        return attend_block(q_block, k_window, v_window, window_mask(start_row, segment, seg_pad, valid_pad, reach))
    blocks = lax.map(jax.checkpoint(one_block), jnp.arange(CAP // MAXLEN, dtype=jnp.int32))
    attn = low_back(low(blocks.reshape(CAP, D)))
    branch = low_back(jnp.dot(attn, out_weight, precision=HIGH) + out_bias)
    middle = tokens_f + branch
    normed_two = low(layer_norm(middle, ln2_gain, ln2_bias))
    pre_act = low_back(jnp.dot(normed_two, fc1_weight, precision=HIGH) + fc1_bias)
    hidden = low(jax.nn.gelu(pre_act))
    result = middle + jnp.dot(hidden, fc2_weight, precision=HIGH) + fc2_bias
    return valid.astype(jnp.float32)[:, None] * result

def reference(tokens, cotangent, seq_lengths, ln1_gain, ln1_bias, qkv_weight, qv_bias, out_weight, out_bias, ln2_gain, ln2_bias, fc1_weight, fc1_bias, fc2_weight, fc2_bias):
    params = tuple((member.astype(jnp.float32) for member in (ln1_gain, ln1_bias, qkv_weight, qv_bias, out_weight, out_bias, ln2_gain, ln2_bias, fc1_weight, fc1_bias, fc2_weight, fc2_bias)))
    inputs = tokens.astype(jnp.float32).reshape(N_DP, CAP, D)
    seeds = cotangent.astype(jnp.float32).reshape(N_DP, CAP, D)

    def per_device(totals, carried):
        tokens_f, cot_rows, lengths = carried
        valid, segment = layout(lengths, CAP)
        output, pullback = jax.vjp(lambda rows_in, weights_in: forward(rows_in, valid, segment, weights_in), tokens_f, params)
        grad_rows, grad_params = pullback(cot_rows)
        return (jax.tree.map(jnp.add, totals, grad_params), (output.astype(jnp.bfloat16), grad_rows))
    totals, (outputs, grad_all) = lax.scan(per_device, tuple((jnp.zeros_like(member) for member in params)), (inputs, seeds, seq_lengths))
    g_ln1_gain, g_ln1_bias, g_qkv, g_qv_bias, g_out, g_out_bias, g_ln2_gain, g_ln2_bias, g_fc1, g_fc1_bias, g_fc2, g_fc2_bias = totals
    return (outputs.reshape(TOKENS, D), grad_all.reshape(TOKENS, D), g_qkv, g_qv_bias, g_out, g_out_bias, g_fc1, g_fc1_bias, g_fc2, g_fc2_bias, g_ln1_gain, g_ln1_bias, g_ln2_gain, g_ln2_bias)
```

```python
import jax
import jax.numpy as jnp
from jax import lax
from jax.experimental import pallas as pl
from jax.experimental.pallas import tpu as pltpu
from jax.sharding import PartitionSpec as P

HEAD_DIM = 64
MAXLEN = 512
PAD = 128


EPS = 1e-05
NEG = -1e30


def normalize(values):
    center = values - jnp.mean(values, axis=-1, keepdims=True)
    inverse = lax.rsqrt(jnp.mean(center * center, axis=-1, keepdims=True) + EPS)
    return (center * inverse, inverse)


def norm_back(grad_out, normed, inverse, gain):
    scaled = grad_out * gain
    return inverse * (
        scaled
        - jnp.mean(scaled, axis=-1, keepdims=True)
        - normed * jnp.mean(scaled * normed, axis=-1, keepdims=True)
    )


def layout(lengths, row_count):
    padded = (lengths + PAD - 1) // PAD * PAD
    starts = jnp.cumsum(padded) - padded
    position = jnp.arange(row_count, dtype=jnp.int32)[:, None]
    inside = (position >= starts[None, :]) & (position < (starts + lengths)[None, :])
    slot_ids = jnp.arange(lengths.shape[0], dtype=jnp.int32)[None, :]
    valid = jnp.any(inside, axis=1)
    chosen = jnp.sum(jnp.where(inside, slot_ids, 0), axis=1)
    return (valid, jnp.where(valid, chosen, -1))


def window_mask(start_row, segment, seg_pad, valid_pad, reach):
    q_pos = start_row + jnp.arange(MAXLEN, dtype=jnp.int32)
    k_pos = start_row - reach + jnp.arange(MAXLEN + reach, dtype=jnp.int32)
    same = (
        valid_pad[None, :]
        & (segment[:, None] == seg_pad[None, :])
        & (k_pos[None, :] <= q_pos[:, None])
    )
    return same | (k_pos[None, :] == q_pos[:, None])


def left_product(left, right):
    return lax.dot_general(
        left, right, (((0,), (0,)), ((), ())), preferred_element_type=jnp.float32
    )


def right_product(left, right):
    return lax.dot_general(
        left, right, (((1,), (1,)), ((), ())), preferred_element_type=jnp.float32
    )


def pack_vectors(members):
    flattened = jnp.concatenate([member.reshape(-1) for member in members])
    return flattened


def unpack_vectors(flattened, members):
    pieces = []
    offset = 0
    for member in members:
        pieces.append(flattened[offset : offset + member.size].reshape(member.shape))
        offset += member.size
    return pieces


def shards(
    tokens,
    cotangent,
    seq_lengths,
    ln1_gain,
    ln1_bias,
    qkv_weight,
    qv_bias,
    out_weight,
    out_bias,
    ln2_gain,
    ln2_bias,
    fc1_weight,
    fc1_bias,
    fc2_weight,
    fc2_bias,
):
    row_count = tokens.shape[0]
    local_width = qkv_weight.shape[2]
    head_count = local_width // HEAD_DIM
    block_count = row_count // MAXLEN
    reach = min(MAXLEN - PAD, row_count - MAXLEN)
    score_scale = HEAD_DIM ** (-0.5)
    share = row_count // lax.axis_size("tensor")
    share_start = lax.axis_index("tensor") * share

    def share_rows(values):
        return lax.dynamic_slice_in_dim(values, share_start, share, 0)

    valid, segment = layout(seq_lengths[0], row_count)
    live = valid.astype(jnp.float32)[:, None]
    seg_pad = jnp.concatenate([jnp.full((reach,), -1, jnp.int32), segment])
    valid_pad = jnp.concatenate([jnp.zeros((reach,), dtype=jnp.bool_), valid])
    block_ids = jnp.arange(block_count, dtype=jnp.int32)
    tokens_f = tokens.astype(jnp.float32)
    norm_one, inverse_one = normalize(tokens_f)
    normed = (norm_one * ln1_gain + ln1_bias).astype(jnp.bfloat16)
    project = jnp.einsum("td,jde->jte", normed, qkv_weight, preferred_element_type=jnp.float32)
    query = (project[0] + qv_bias[0]).astype(jnp.bfloat16).reshape(row_count, head_count, HEAD_DIM)
    keys_all = project[1].astype(jnp.bfloat16).reshape(row_count, head_count, HEAD_DIM)
    values_all = (
        (project[2] + qv_bias[1]).astype(jnp.bfloat16).reshape(row_count, head_count, HEAD_DIM)
    )
    blank = jnp.zeros((reach, head_count, HEAD_DIM), jnp.bfloat16)
    key_pad = jnp.concatenate([blank, keys_all], axis=0)
    value_pad = jnp.concatenate([blank, values_all], axis=0)

    def window(block_index):
        start_row = block_index * MAXLEN
        allowed = window_mask(start_row, segment, seg_pad, valid_pad, reach)
        scores = (
            jnp.einsum("qhd,khd->hqk", query, key_pad, preferred_element_type=jnp.float32)
            * score_scale
        )
        return (start_row, query, key_pad, value_pad, jnp.where(allowed[None], scores, NEG))

    def attend(block_index):
        start_row, q_block, k_window, v_window, scores = window(block_index)
        row_max = jnp.max(scores, axis=-1, keepdims=True)
        weights = jnp.exp(scores - row_max)
        totals = jnp.sum(weights, axis=-1, keepdims=True)
        prob = (weights / totals).astype(jnp.bfloat16)
        mixed = jnp.einsum("hqk,khd->qhd", prob, v_window, preferred_element_type=jnp.float32)
        return (mixed.astype(jnp.bfloat16), row_max + jnp.log(totals))

    attn_blocks, log_norm = lax.map(attend, block_ids)
    attn = attn_blocks.reshape(row_count, local_width)
    middle = (
        share_rows(tokens_f)
        + lax.psum_scatter(
            jnp.dot(attn, out_weight, preferred_element_type=jnp.float32),
            "tensor",
            scatter_dimension=0,
            tiled=True,
        )
        + out_bias
    )
    norm_two, inverse_two = normalize(middle)
    normed_share = (norm_two * ln2_gain + ln2_bias).astype(jnp.bfloat16)
    normed_two = lax.all_gather(normed_share, "tensor", axis=0, tiled=True)
    pre_act = jnp.dot(normed_two, fc1_weight, preferred_element_type=jnp.float32) + fc1_bias
    hidden = jax.nn.gelu(pre_act).astype(jnp.bfloat16)
    result = (
        middle
        + lax.psum_scatter(
            jnp.dot(hidden, fc2_weight, preferred_element_type=jnp.float32).astype(jnp.bfloat16),
            "tensor",
            scatter_dimension=0,
            tiled=True,
        ).astype(jnp.float32)
        + fc2_bias
    )
    block_out = (share_rows(live) * result).astype(jnp.bfloat16)
    grad_y = cotangent * live.astype(jnp.bfloat16)
    grad_y_f = grad_y.astype(jnp.float32)
    fc2_grad = left_product(hidden, grad_y)
    fc2_bias_grad = jnp.sum(grad_y_f, axis=0)
    grad_hidden = right_product(grad_y, fc2_weight)
    grad_pre = jax.vjp(jax.nn.gelu, pre_act)[1](grad_hidden)[0].astype(jnp.bfloat16)
    fc1_grad = left_product(normed_two, grad_pre)
    fc1_bias_grad = jnp.sum(grad_pre.astype(jnp.float32), axis=0)
    grad_norm_two = lax.psum_scatter(
        right_product(grad_pre, fc1_weight), "tensor", scatter_dimension=0, tiled=True
    )
    ln2_gain_part = jnp.sum(grad_norm_two * norm_two, axis=0)
    ln2_bias_part = jnp.sum(grad_norm_two, axis=0)
    grad_middle = share_rows(grad_y_f) + norm_back(grad_norm_two, norm_two, inverse_two, ln2_gain)
    grad_branch = lax.all_gather(grad_middle.astype(jnp.bfloat16), "tensor", axis=0, tiled=True)
    out_bias_grad = jnp.sum(grad_branch.astype(jnp.float32), axis=0)
    out_grad = left_product(attn, grad_branch)
    grad_attn = (
        right_product(grad_branch, out_weight)
        .astype(jnp.bfloat16)
        .reshape(row_count, head_count, HEAD_DIM)
    )
    zero_pad = jnp.zeros((row_count + reach, head_count, HEAD_DIM), jnp.float32)

    def attend_back(running, block_index):
        key_grad, value_grad = running
        start_row, q_block, k_window, v_window, scores = window(block_index)
        prob = jnp.exp(scores - log_norm[block_index])
        value_part = jnp.einsum(
            "hqk,qhd->khd", prob.astype(jnp.bfloat16), grad_attn, preferred_element_type=jnp.float32
        )
        grad_prob = jnp.einsum(
            "qhd,khd->hqk", grad_attn, v_window, preferred_element_type=jnp.float32
        )
        centre = jnp.sum(prob * grad_prob, axis=-1, keepdims=True)
        grad_score = (prob * (grad_prob - centre)).astype(jnp.bfloat16)
        query_part = (
            jnp.einsum("hqk,khd->qhd", grad_score, k_window, preferred_element_type=jnp.float32)
            * score_scale
        )
        key_part = (
            jnp.einsum("hqk,qhd->khd", grad_score, q_block, preferred_element_type=jnp.float32)
            * score_scale
        )
        key_grad = key_grad + key_part
        value_grad = value_grad + value_part
        return ((key_grad, value_grad), query_part)

    (key_grad, value_grad), query_parts = lax.scan(attend_back, (zero_pad, zero_pad), block_ids)
    grad_query = query_parts.reshape(row_count, local_width).astype(jnp.bfloat16)
    grad_key = key_grad.reshape(row_count, local_width).astype(jnp.bfloat16)
    grad_value = value_grad.reshape(row_count, local_width).astype(jnp.bfloat16)
    stacked = jnp.stack([grad_query, grad_key, grad_value])
    qkv_grad = jnp.einsum("td,jte->jde", normed, stacked, preferred_element_type=jnp.float32)
    qv_bias_grad = jnp.stack(
        [
            jnp.sum(grad_query.astype(jnp.float32), axis=0),
            jnp.sum(grad_value.astype(jnp.float32), axis=0),
        ]
    )
    grad_normed = lax.psum_scatter(
        jnp.einsum("jte,jde->td", stacked, qkv_weight, preferred_element_type=jnp.float32).astype(
            jnp.bfloat16
        ),
        "tensor",
        scatter_dimension=0,
        tiled=True,
    ).astype(jnp.float32)
    norm_one_share = share_rows(norm_one)
    ln1_gain_part = jnp.sum(grad_normed * norm_one_share, axis=0)
    ln1_bias_part = jnp.sum(grad_normed, axis=0)
    tokens_grad = grad_middle + norm_back(
        grad_normed, norm_one_share, share_rows(inverse_one), ln1_gain
    )
    ln1_gain_grad, ln1_bias_grad, ln2_gain_grad, ln2_bias_grad = lax.psum(
        (ln1_gain_part, ln1_bias_part, ln2_gain_part, ln2_bias_part), "tensor"
    )
    vectors = (
        qv_bias_grad,
        out_bias_grad,
        fc1_bias_grad,
        fc2_bias_grad,
        ln1_gain_grad,
        ln1_bias_grad,
        ln2_gain_grad,
        ln2_bias_grad,
    )
    flattened = pack_vectors(vectors)
    qkv_sum, out_sum, fc1_sum, fc2_sum, flat_sum = (
        lax.psum_scatter(qkv_grad, "dp", scatter_dimension=1, tiled=True),
        lax.psum_scatter(out_grad, "dp", scatter_dimension=1, tiled=True),
        lax.psum_scatter(fc1_grad, "dp", scatter_dimension=0, tiled=True),
        lax.psum_scatter(fc2_grad, "dp", scatter_dimension=1, tiled=True),
        lax.psum_scatter(flattened, "dp", scatter_dimension=0, tiled=True),
    )
    summed = unpack_vectors(lax.all_gather(flat_sum, "dp", axis=0, tiled=True), vectors)
    return (
        block_out,
        tokens_grad,
        qkv_sum,
        summed[0],
        out_sum,
        summed[1],
        fc1_sum,
        summed[2],
        fc2_sum,
        summed[3],
        summed[4],
        summed[5],
        summed[6],
        summed[7],
    )


MESH = pl.DeviceIdType.MESH
BF16 = jnp.bfloat16
F32 = jnp.float32
GROUP = 4
SLOT = 256


def plain(left, right):
    return jnp.dot(left, right, preferred_element_type=F32)


def column_sum(values):
    return jnp.sum(values, axis=0, keepdims=True)


def layer_kernel(
    tokens, cotangent, lengths, ln1_gain, ln1_bias, qkv_weight, qv_bias, out_weight, out_bias,
    ln2_gain, ln2_bias, fc1_weight, fc1_bias, fc2_weight, fc2_bias,
    block_out, tokens_grad, fc1_out, fc2_out, out_out, qkv_out, vector_out,
    norm_one, inverse_one, normed, query, keys, values, probs, attn, weights_all,
    middle, norm_two, inverse_two, normed_two, hidden, grad_pre, grad_y,
    part_two, from_two, part_y, from_y, branch, grad_middle, grad_attn,
    key_sum, value_sum, stacked, part_one, from_one,
    own, from_x, summed, from_z, vector, vec_t, vec_x, vec_z,
    e0_send, e0_recv, e1_send, e1_recv, e2_send, e2_recv, e3_send, e3_recv,
    e4_send, e4_recv, e5_send, e5_recv, x_send, x_recv, z_send, z_recv,
    vt_send, vt_recv, vx_send, vx_recv, vz_send, vz_recv,
):
    share = tokens.shape[0] // GROUP
    width = qkv_weight.shape[2]
    heads = width // HEAD_DIM
    scale = HEAD_DIM ** (-0.5)
    steps = own[0].shape[0]
    t = lax.axis_index("tensor")
    d = lax.axis_index("dp")
    z, x = d // 2, d % 2
    other = d + 1 - 2 * x
    peers = [lax.rem(t + s, GROUP) for s in range(1, GROUP)]
    zs = [lax.rem(z + s, steps) for s in range(1, steps)]

    barrier = pltpu.get_barrier_semaphore()
    for peer in peers:
        pl.semaphore_signal(barrier, inc=1, device_id={"tensor": peer}, device_id_type=MESH)
    pl.semaphore_signal(barrier, inc=1, device_id={"dp": other}, device_id_type=MESH)
    for to in zs:
        pl.semaphore_signal(barrier, inc=1, device_id={"dp": 2 * to + x}, device_id_type=MESH)
    pl.semaphore_wait(barrier, len(peers) + 1 + len(zs))

    def remote(src, dst, send, recv, **target):
        return pltpu.make_async_remote_copy(
            src_ref=src, dst_ref=dst, send_sem=send, recv_sem=recv,
            device_id=target, device_id_type=MESH,
        )

    pending = []

    def begin(copy):
        copy.start()
        pending.append(copy)

    def rows(i):
        return pl.ds(share * i, share)

    weights_all[t] = out_weight[...]
    for s, peer in enumerate(peers):
        begin(remote(weights_all.at[t], weights_all.at[t], e0_send.at[s], e0_recv.at[t], tensor=peer))

    length = lengths[0, 0]
    column = lax.broadcasted_iota(jnp.int32, (1, width), 1) // HEAD_DIM
    picks = [(column == h).astype(BF16) for h in range(heads)]
    vector[...] = jnp.zeros_like(vector)

    for i in range(GROUP):
        n, inverse = normalize(tokens[rows(i), :].astype(F32))
        norm_one[rows(i), :] = n
        inverse_one[rows(i), :] = inverse
        low = (n * ln1_gain[...] + ln1_bias[...]).astype(BF16)
        normed[rows(i), :] = low
        query[rows(i), :] = (plain(low, qkv_weight[0]) + qv_bias[0:1, :]).astype(BF16)
        keys[rows(i), :] = plain(low, qkv_weight[1]).astype(BF16)
        values[rows(i), :] = (plain(low, qkv_weight[2]) + qv_bias[1:2, :]).astype(BF16)
        live = lax.broadcasted_iota(jnp.int32, (share, 1), 0) + share * i < length
        g = cotangent[rows(i), :].astype(F32) * live.astype(F32)
        grad_y[rows(i), :] = g.astype(BF16)
        vector[9:10, :] += column_sum(g)

    for i in range(GROUP):
        span = share * (i + 1)
        row = lax.broadcasted_iota(jnp.int32, (share, span), 0) + share * i
        col = lax.broadcasted_iota(jnp.int32, (share, span), 1)
        allowed = ((col <= row) & (row < length)) | (col == row)
        mixed = jnp.zeros((share, width), F32)
        k, v = keys[0:span, :], values[0:span, :]
        for h in range(heads):
            scores = right_product(query[rows(i), :] * picks[h], k) * scale
            scores = jnp.where(allowed, scores, NEG)
            e = jnp.exp(scores - jnp.max(scores, axis=-1, keepdims=True))
            p = e / jnp.sum(e, axis=-1, keepdims=True)
            probs[h, rows(i), 0:span] = p
            mixed += plain(p.astype(BF16), v * picks[h])
        attn[t, rows(i), :] = mixed.astype(BF16)
        for s, peer in enumerate(peers):
            begin(remote(
                attn.at[t, rows(i)], attn.at[t, rows(i)],
                e1_send.at[i, s], e1_recv.at[i, t], tensor=peer,
            ))

    for s, peer in enumerate(peers):
        remote(weights_all.at[peer], weights_all.at[peer], e0_send.at[s], e0_recv.at[peer], tensor=peer).wait_recv()

    def send_share(i, part, landing, send, recv):
        @pl.when(t != i)
        def _():
            remote(part.at[i], landing.at[t], send.at[i], recv.at[t], tensor=i).start()

    def sum_shares(part, landing, send, recv):
        for peer in peers:
            remote(part.at[peer], landing.at[peer], send.at[peer], recv.at[peer], tensor=peer).wait()
        total = part[t].astype(F32)
        for peer in peers:
            total += landing[peer].astype(F32)
        return total

    curve = (2.0 / jnp.pi) ** 0.5
    for i in range(GROUP):
        for s, peer in enumerate(peers):
            remote(
                attn.at[peer, rows(i)], attn.at[peer, rows(i)],
                e1_send.at[i, s], e1_recv.at[i, peer], tensor=peer,
            ).wait_recv()
        mid = tokens[rows(i), :].astype(F32) + out_bias[...]
        for u in range(GROUP):
            mid += plain(attn[u, rows(i), :], weights_all[u])
        middle[rows(i), :] = mid
        n, inverse = normalize(mid)
        norm_two[rows(i), :] = n
        inverse_two[rows(i), :] = inverse
        low = (n * ln2_gain[...] + ln2_bias[...]).astype(BF16)
        normed_two[rows(i), :] = low
        pre = plain(low, fc1_weight[...]) + fc1_bias[...]
        square = pre * pre
        th = jnp.tanh(curve * (pre + 0.044715 * square * pre))
        half = 0.5 * (1.0 + th)
        hidden[rows(i), :] = (pre * half).astype(BF16)
        slope = half + 0.5 * pre * (1.0 - th * th) * (curve * (1.0 + 0.134145 * square))
        gp = (slope * right_product(grad_y[rows(i), :], fc2_weight[...])).astype(BF16)
        grad_pre[rows(i), :] = gp
        vector[10:11, :] += column_sum(gp.astype(F32))
        gn = right_product(gp, fc1_weight[...])
        vector[2:3, :] += column_sum(gn * n)
        vector[3:4, :] += column_sum(gn)
        part_two[i] = gn.astype(BF16)
        send_share(i, part_two, from_two, e2_send, e2_recv)

    def x_copy(p):
        return remote(own[p].at[:, 1 - x], from_x[p], x_send.at[p], x_recv.at[p], dp=other)

    def x_start(p, grad):
        own[p][...] = grad.astype(BF16).reshape(own[p].shape)
        x_copy(p).start()

    def z_copy(p, s):
        return remote(
            summed[p].at[zs[s]], from_z[p].at[s], z_send.at[p, s], z_recv.at[p, s],
            dp=2 * zs[s] + x,
        )

    def z_start(p):
        x_copy(p).wait()
        for k in range(steps):
            summed[p][k] = (own[p][k, x].astype(F32) + from_x[p][k].astype(F32)).astype(BF16)
        for s in range(steps - 1):
            z_copy(p, s).start()

    def z_finish(p):
        total = summed[p][z].astype(F32)
        for s in range(steps - 1):
            z_copy(p, s).wait()
            total += from_z[p][s].astype(F32)
        return total

    x_start(0, left_product(grad_y[...], hidden[...]))
    for i in range(GROUP):
        part_y[i] = plain(hidden[rows(i), :], fc2_weight[...]).astype(BF16)
        send_share(i, part_y, from_y, e5_send, e5_recv)

    mine = pl.ds(pl.multiple_of(share * t, share), share)
    gn = sum_shares(part_two, from_two, e2_send, e2_recv)
    position = lax.broadcasted_iota(jnp.int32, (share, 1), 0) + share * t
    live = (position < length).astype(F32)
    gm = grad_y[mine, :].astype(F32) + norm_back(gn, norm_two[mine, :], inverse_two[mine, :], ln2_gain[...])
    grad_middle[...] = gm
    branch[t] = gm.astype(BF16)
    for s, peer in enumerate(peers):
        begin(remote(branch.at[t], branch.at[t], e3_send.at[s], e3_recv.at[t], tensor=peer))

    x_start(1, left_product(normed_two[...], grad_pre[...]))
    result = middle[mine, :] + sum_shares(part_y, from_y, e5_send, e5_recv) + fc2_bias[...]
    block_out[...] = (live * result).astype(BF16)
    z_start(0)

    for s, peer in enumerate(peers):
        remote(branch.at[peer], branch.at[peer], e3_send.at[s], e3_recv.at[peer], tensor=peer).wait_recv()
    for i in range(GROUP):
        grad_attn[rows(i), :] = right_product(branch[i], out_weight[...]).astype(BF16)
        vector[8:9, :] += column_sum(branch[i].astype(F32))
    x_start(2, left_product(branch[...].reshape(tokens.shape), attn[t]))

    key_sum[...] = jnp.zeros_like(key_sum)
    value_sum[...] = jnp.zeros_like(value_sum)
    for i in range(GROUP):
        span = share * (i + 1)
        k, v = keys[0:span, :], values[0:span, :]
        query_sum = jnp.zeros((share, width), F32)
        for h in range(heads):
            p = probs[h, rows(i), 0:span]
            ga = grad_attn[rows(i), :] * picks[h]
            gprob = right_product(ga, v)
            centre = jnp.sum(p * gprob, axis=-1, keepdims=True)
            gs = (p * (gprob - centre)).astype(BF16)
            query_sum += plain(gs, k * picks[h])
            key_sum[0:span, :] += left_product(gs, query[rows(i), :] * picks[h])
            value_sum[0:span, :] += left_product(p.astype(BF16), ga)
        stacked[rows(i), 0:width] = (query_sum * scale).astype(BF16)
    stacked[:, SLOT : SLOT + width] = (key_sum[...] * scale).astype(BF16)
    stacked[:, 2 * SLOT : 2 * SLOT + width] = value_sum[...].astype(BF16)
    for j in range(3):
        x_start(3 + j, left_product(normed[...], stacked[:, SLOT * j : SLOT * j + width]))

    vector[11:12, 0:width] = column_sum(stacked[:, 0:width].astype(F32))
    vector[12:13, 0:width] = column_sum(stacked[:, 2 * SLOT : 2 * SLOT + width].astype(F32))
    for i in range(GROUP):
        gn = jnp.zeros((share, tokens.shape[1]), F32)
        for j in range(3):
            gn += right_product(stacked[rows(i), SLOT * j : SLOT * j + width], qkv_weight[j])
        vector[0:1, :] += column_sum(gn * norm_one[rows(i), :])
        vector[1:2, :] += column_sum(gn)
        part_one[i] = gn.astype(BF16)
        send_share(i, part_one, from_one, e4_send, e4_recv)

    vec_t[t] = vector[0:8, :]
    for s, peer in enumerate(peers):
        begin(remote(vec_t.at[t], vec_t.at[t], vt_send.at[s], vt_recv.at[t], tensor=peer))
    z_start(1)
    z_start(2)
    for s, peer in enumerate(peers):
        remote(vec_t.at[peer], vec_t.at[peer], vt_send.at[s], vt_recv.at[peer], tensor=peer).wait_recv()
    vector[0:8, :] = vec_t[0] + vec_t[1] + vec_t[2] + vec_t[3]
    pair = remote(vector, vec_x, vx_send, vx_recv, dp=other)
    pair.start()
    for j in range(3):
        z_start(3 + j)
    pair.wait()
    vec_z[z] = vector[...] + vec_x[...]
    for s, to in enumerate(zs):
        begin(remote(vec_z.at[z], vec_z.at[z], vz_send.at[s], vz_recv.at[z], dp=2 * to + x))

    gn = sum_shares(part_one, from_one, e4_send, e4_recv)
    tokens_grad[...] = grad_middle[...] + norm_back(
        gn, norm_one[mine, :], inverse_one[mine, :], ln1_gain[...]
    )
    fc2_out[...] = z_finish(0)
    fc1_out[...] = z_finish(1)
    out_out[...] = z_finish(2)
    for j in range(3):
        qkv_out[j] = z_finish(3 + j)
    for s, to in enumerate(zs):
        remote(vec_z.at[to], vec_z.at[to], vz_send.at[s], vz_recv.at[to], dp=2 * to + x).wait_recv()
    total = vec_z[0]
    for k in range(1, steps):
        total += vec_z[k]
    vector_out[...] = total
    for copy in pending:
        copy.wait_send()


def fused(
    tokens, cotangent, seq_lengths, ln1_gain, ln1_bias, qkv_weight, qv_bias, out_weight, out_bias,
    ln2_gain, ln2_bias, fc1_weight, fc1_bias, fc2_weight, fc2_bias,
):
    count, depth = tokens.shape
    width = qkv_weight.shape[2]
    units = fc1_weight.shape[1]
    heads = width // HEAD_DIM
    share = count // GROUP
    members = lax.axis_size("dp")
    steps = members // 2
    chunk = depth // members
    widths = (units, units, width, width, width, width)
    vmem = pltpu.VMEM
    dma = pltpu.SemaphoreType.DMA
    parts = len(widths)
    scratch = [
        vmem((count, depth), F32), vmem((count, 1), F32), vmem((count, depth), BF16),
        vmem((count, width), BF16), vmem((count, width), BF16), vmem((count, width), BF16),
        vmem((heads, count, count), F32),
        vmem((GROUP, count, width), BF16), vmem((GROUP, width, depth), BF16),
        vmem((count, depth), F32), vmem((count, depth), F32), vmem((count, 1), F32),
        vmem((count, depth), BF16), vmem((count, units), BF16), vmem((count, units), BF16),
        vmem((count, depth), BF16),
        vmem((GROUP, share, depth), BF16), vmem((GROUP, share, depth), BF16),
        vmem((GROUP, share, depth), BF16), vmem((GROUP, share, depth), BF16),
        vmem((GROUP, share, depth), BF16), vmem((share, depth), F32), vmem((count, width), BF16),
        vmem((count, width), F32), vmem((count, width), F32), vmem((count, 3 * SLOT), BF16),
        vmem((GROUP, share, depth), BF16), vmem((GROUP, share, depth), BF16),
        [vmem((steps, 2, chunk, w), BF16) for w in widths],
        [vmem((steps, chunk, w), BF16) for w in widths],
        [vmem((steps, chunk, w), BF16) for w in widths],
        [vmem((steps - 1, chunk, w), BF16) for w in widths],
        vmem((16, depth), F32), vmem((GROUP, 8, depth), F32), vmem((16, depth), F32),
        vmem((steps, 16, depth), F32),
        dma((GROUP - 1,)), dma((GROUP,)),
        dma((GROUP, GROUP - 1)), dma((GROUP, GROUP)),
        dma((GROUP,)), dma((GROUP,)),
        dma((GROUP - 1,)), dma((GROUP,)),
        dma((GROUP,)), dma((GROUP,)),
        dma((GROUP,)), dma((GROUP,)),
        dma((parts,)), dma((parts,)),
        dma((parts, steps - 1)), dma((parts, steps - 1)),
        dma((GROUP - 1,)), dma((GROUP,)),
        dma, dma,
        dma((steps - 1,)), dma((steps,)),
    ]
    in_vmem = pl.BlockSpec(memory_space=pltpu.VMEM)
    shape = jax.ShapeDtypeStruct
    line = lambda value: value.reshape(1, -1)
    block, grad, fc1, fc2, out, qkv, vec = pl.pallas_call(
        layer_kernel,
        out_shape=(
            shape((share, depth), BF16), shape((share, depth), F32), shape((chunk, units), F32),
            shape((chunk, units), F32), shape((chunk, width), F32), shape((3, chunk, width), F32),
            shape((16, depth), F32),
        ),
        in_specs=[in_vmem] * 2 + [pl.BlockSpec(memory_space=pltpu.SMEM)] + [in_vmem] * 12,
        out_specs=(in_vmem,) * 7,
        scratch_shapes=scratch,
        compiler_params=pltpu.CompilerParams(
            collective_id=0, has_side_effects=True, vmem_limit_bytes=56 * 2**20
        ),
        name="layer",
    )(
        tokens, cotangent, seq_lengths, line(ln1_gain), line(ln1_bias), qkv_weight, qv_bias,
        out_weight, line(out_bias), line(ln2_gain), line(ln2_bias), fc1_weight, line(fc1_bias),
        fc2_weight, line(fc2_bias),
    )
    return (
        block, grad, qkv, vec[11:13, :width], out.T, vec[8], fc1, vec[10], fc2.T, vec[9],
        vec[0], vec[1], vec[2], vec[3],
    )


def layer(*arguments):
    count, depth = arguments[0].shape
    members = lax.axis_size("dp")
    fits = (
        lax.axis_size("tensor") == GROUP
        and count == MAXLEN
        and arguments[2].shape[1] == 1
        and members % 2 == 0
        and depth % (16 * members) == 0
        and arguments[11].shape[1] == depth
    )
    return fused(*arguments) if fits else shards(*arguments)


def solution(mesh):
    placed = (
        P("dp", None),
        P("dp", None),
        P("dp", None),
        P(),
        P(),
        P(None, None, "tensor"),
        P(None, "tensor"),
        P("tensor", None),
        P(),
        P(),
        P(),
        P(None, "tensor"),
        P("tensor"),
        P("tensor", None),
        P(),
    )
    return jax.shard_map(
        layer,
        mesh=mesh,
        in_specs=placed,
        out_specs=(
            P(("dp", "tensor"), None),
            P(("dp", "tensor"), None),
            P(None, "dp", "tensor"),
            P(None, "tensor"),
            P("tensor", "dp"),
            P(),
            P("dp", "tensor"),
            P("tensor"),
            P("tensor", "dp"),
            P(),
            P(),
            P(),
            P(),
            P(),
        ),
        check_vma=False,
    )
```

```python
import jax
import jax.numpy as jnp
from jax import lax
from jax.experimental import pallas as pl
from jax.experimental.pallas import tpu as pltpu
from jax.sharding import PartitionSpec as P

HEAD_DIM = 64
MAXLEN = 512
PAD = 128


EPS = 1e-05
NEG = -1e30


def normalize(values):
    center = values - jnp.mean(values, axis=-1, keepdims=True)
    inverse = lax.rsqrt(jnp.mean(center * center, axis=-1, keepdims=True) + EPS)
    return (center * inverse, inverse)


def norm_back(grad_out, normed, inverse, gain):
    scaled = grad_out * gain
    return inverse * (
        scaled
        - jnp.mean(scaled, axis=-1, keepdims=True)
        - normed * jnp.mean(scaled * normed, axis=-1, keepdims=True)
    )


def layout(lengths, row_count):
    padded = (lengths + PAD - 1) // PAD * PAD
    starts = jnp.cumsum(padded) - padded
    position = jnp.arange(row_count, dtype=jnp.int32)[:, None]
    inside = (position >= starts[None, :]) & (position < (starts + lengths)[None, :])
    slot_ids = jnp.arange(lengths.shape[0], dtype=jnp.int32)[None, :]
    valid = jnp.any(inside, axis=1)
    chosen = jnp.sum(jnp.where(inside, slot_ids, 0), axis=1)
    return (valid, jnp.where(valid, chosen, -1))


def window_mask(start_row, segment, seg_pad, valid_pad, reach):
    q_pos = start_row + jnp.arange(MAXLEN, dtype=jnp.int32)
    k_pos = start_row - reach + jnp.arange(MAXLEN + reach, dtype=jnp.int32)
    same = (
        valid_pad[None, :]
        & (segment[:, None] == seg_pad[None, :])
        & (k_pos[None, :] <= q_pos[:, None])
    )
    return same | (k_pos[None, :] == q_pos[:, None])


def left_product(left, right):
    return lax.dot_general(
        left, right, (((0,), (0,)), ((), ())), preferred_element_type=jnp.float32
    )


def right_product(left, right):
    return lax.dot_general(
        left, right, (((1,), (1,)), ((), ())), preferred_element_type=jnp.float32
    )


def pack_vectors(members):
    flattened = jnp.concatenate([member.reshape(-1) for member in members])
    return flattened


def unpack_vectors(flattened, members):
    pieces = []
    offset = 0
    for member in members:
        pieces.append(flattened[offset : offset + member.size].reshape(member.shape))
        offset += member.size
    return pieces


def shards(
    tokens,
    cotangent,
    seq_lengths,
    ln1_gain,
    ln1_bias,
    qkv_weight,
    qv_bias,
    out_weight,
    out_bias,
    ln2_gain,
    ln2_bias,
    fc1_weight,
    fc1_bias,
    fc2_weight,
    fc2_bias,
):
    row_count = tokens.shape[0]
    local_width = qkv_weight.shape[2]
    head_count = local_width // HEAD_DIM
    block_count = row_count // MAXLEN
    reach = min(MAXLEN - PAD, row_count - MAXLEN)
    score_scale = HEAD_DIM ** (-0.5)
    share = row_count // lax.axis_size("tensor")
    share_start = lax.axis_index("tensor") * share

    def share_rows(values):
        return lax.dynamic_slice_in_dim(values, share_start, share, 0)

    valid, segment = layout(seq_lengths[0], row_count)
    live = valid.astype(jnp.float32)[:, None]
    seg_pad = jnp.concatenate([jnp.full((reach,), -1, jnp.int32), segment])
    valid_pad = jnp.concatenate([jnp.zeros((reach,), dtype=jnp.bool_), valid])
    block_ids = jnp.arange(block_count, dtype=jnp.int32)
    tokens_f = tokens.astype(jnp.float32)
    norm_one, inverse_one = normalize(tokens_f)
    normed = (norm_one * ln1_gain + ln1_bias).astype(jnp.bfloat16)
    project = jnp.einsum("td,jde->jte", normed, qkv_weight, preferred_element_type=jnp.float32)
    query = (project[0] + qv_bias[0]).astype(jnp.bfloat16).reshape(row_count, head_count, HEAD_DIM)
    keys_all = project[1].astype(jnp.bfloat16).reshape(row_count, head_count, HEAD_DIM)
    values_all = (
        (project[2] + qv_bias[1]).astype(jnp.bfloat16).reshape(row_count, head_count, HEAD_DIM)
    )
    blank = jnp.zeros((reach, head_count, HEAD_DIM), jnp.bfloat16)
    key_pad = jnp.concatenate([blank, keys_all], axis=0)
    value_pad = jnp.concatenate([blank, values_all], axis=0)

    def window(block_index):
        start_row = block_index * MAXLEN
        allowed = window_mask(start_row, segment, seg_pad, valid_pad, reach)
        scores = (
            jnp.einsum("qhd,khd->hqk", query, key_pad, preferred_element_type=jnp.float32)
            * score_scale
        )
        return (start_row, query, key_pad, value_pad, jnp.where(allowed[None], scores, NEG))

    def attend(block_index):
        start_row, q_block, k_window, v_window, scores = window(block_index)
        row_max = jnp.max(scores, axis=-1, keepdims=True)
        weights = jnp.exp(scores - row_max)
        totals = jnp.sum(weights, axis=-1, keepdims=True)
        prob = (weights / totals).astype(jnp.bfloat16)
        mixed = jnp.einsum("hqk,khd->qhd", prob, v_window, preferred_element_type=jnp.float32)
        return (mixed.astype(jnp.bfloat16), row_max + jnp.log(totals))

    attn_blocks, log_norm = lax.map(attend, block_ids)
    attn = attn_blocks.reshape(row_count, local_width)
    middle = (
        share_rows(tokens_f)
        + lax.psum_scatter(
            jnp.dot(attn, out_weight, preferred_element_type=jnp.float32),
            "tensor",
            scatter_dimension=0,
            tiled=True,
        )
        + out_bias
    )
    norm_two, inverse_two = normalize(middle)
    normed_share = (norm_two * ln2_gain + ln2_bias).astype(jnp.bfloat16)
    normed_two = lax.all_gather(normed_share, "tensor", axis=0, tiled=True)
    pre_act = jnp.dot(normed_two, fc1_weight, preferred_element_type=jnp.float32) + fc1_bias
    hidden = jax.nn.gelu(pre_act).astype(jnp.bfloat16)
    result = (
        middle
        + lax.psum_scatter(
            jnp.dot(hidden, fc2_weight, preferred_element_type=jnp.float32).astype(jnp.bfloat16),
            "tensor",
            scatter_dimension=0,
            tiled=True,
        ).astype(jnp.float32)
        + fc2_bias
    )
    block_out = (share_rows(live) * result).astype(jnp.bfloat16)
    grad_y = cotangent * live.astype(jnp.bfloat16)
    grad_y_f = grad_y.astype(jnp.float32)
    fc2_grad = left_product(hidden, grad_y)
    fc2_bias_grad = jnp.sum(grad_y_f, axis=0)
    grad_hidden = right_product(grad_y, fc2_weight)
    grad_pre = jax.vjp(jax.nn.gelu, pre_act)[1](grad_hidden)[0].astype(jnp.bfloat16)
    fc1_grad = left_product(normed_two, grad_pre)
    fc1_bias_grad = jnp.sum(grad_pre.astype(jnp.float32), axis=0)
    grad_norm_two = lax.psum_scatter(
        right_product(grad_pre, fc1_weight), "tensor", scatter_dimension=0, tiled=True
    )
    ln2_gain_part = jnp.sum(grad_norm_two * norm_two, axis=0)
    ln2_bias_part = jnp.sum(grad_norm_two, axis=0)
    grad_middle = share_rows(grad_y_f) + norm_back(grad_norm_two, norm_two, inverse_two, ln2_gain)
    grad_branch = lax.all_gather(grad_middle.astype(jnp.bfloat16), "tensor", axis=0, tiled=True)
    out_bias_grad = jnp.sum(grad_branch.astype(jnp.float32), axis=0)
    out_grad = left_product(attn, grad_branch)
    grad_attn = (
        right_product(grad_branch, out_weight)
        .astype(jnp.bfloat16)
        .reshape(row_count, head_count, HEAD_DIM)
    )
    zero_pad = jnp.zeros((row_count + reach, head_count, HEAD_DIM), jnp.float32)

    def attend_back(running, block_index):
        key_grad, value_grad = running
        start_row, q_block, k_window, v_window, scores = window(block_index)
        prob = jnp.exp(scores - log_norm[block_index])
        value_part = jnp.einsum(
            "hqk,qhd->khd", prob.astype(jnp.bfloat16), grad_attn, preferred_element_type=jnp.float32
        )
        grad_prob = jnp.einsum(
            "qhd,khd->hqk", grad_attn, v_window, preferred_element_type=jnp.float32
        )
        centre = jnp.sum(prob * grad_prob, axis=-1, keepdims=True)
        grad_score = (prob * (grad_prob - centre)).astype(jnp.bfloat16)
        query_part = (
            jnp.einsum("hqk,khd->qhd", grad_score, k_window, preferred_element_type=jnp.float32)
            * score_scale
        )
        key_part = (
            jnp.einsum("hqk,qhd->khd", grad_score, q_block, preferred_element_type=jnp.float32)
            * score_scale
        )
        key_grad = key_grad + key_part
        value_grad = value_grad + value_part
        return ((key_grad, value_grad), query_part)

    (key_grad, value_grad), query_parts = lax.scan(attend_back, (zero_pad, zero_pad), block_ids)
    grad_query = query_parts.reshape(row_count, local_width).astype(jnp.bfloat16)
    grad_key = key_grad.reshape(row_count, local_width).astype(jnp.bfloat16)
    grad_value = value_grad.reshape(row_count, local_width).astype(jnp.bfloat16)
    stacked = jnp.stack([grad_query, grad_key, grad_value])
    qkv_grad = jnp.einsum("td,jte->jde", normed, stacked, preferred_element_type=jnp.float32)
    qv_bias_grad = jnp.stack(
        [
            jnp.sum(grad_query.astype(jnp.float32), axis=0),
            jnp.sum(grad_value.astype(jnp.float32), axis=0),
        ]
    )
    grad_normed = lax.psum_scatter(
        jnp.einsum("jte,jde->td", stacked, qkv_weight, preferred_element_type=jnp.float32).astype(
            jnp.bfloat16
        ),
        "tensor",
        scatter_dimension=0,
        tiled=True,
    ).astype(jnp.float32)
    norm_one_share = share_rows(norm_one)
    ln1_gain_part = jnp.sum(grad_normed * norm_one_share, axis=0)
    ln1_bias_part = jnp.sum(grad_normed, axis=0)
    tokens_grad = grad_middle + norm_back(
        grad_normed, norm_one_share, share_rows(inverse_one), ln1_gain
    )
    ln1_gain_grad, ln1_bias_grad, ln2_gain_grad, ln2_bias_grad = lax.psum(
        (ln1_gain_part, ln1_bias_part, ln2_gain_part, ln2_bias_part), "tensor"
    )
    vectors = (
        qv_bias_grad,
        out_bias_grad,
        fc1_bias_grad,
        fc2_bias_grad,
        ln1_gain_grad,
        ln1_bias_grad,
        ln2_gain_grad,
        ln2_bias_grad,
    )
    flattened = pack_vectors(vectors)
    qkv_sum, out_sum, fc1_sum, fc2_sum, flat_sum = (
        lax.psum_scatter(qkv_grad, "dp", scatter_dimension=1, tiled=True),
        lax.psum_scatter(out_grad, "dp", scatter_dimension=1, tiled=True),
        lax.psum_scatter(fc1_grad, "dp", scatter_dimension=0, tiled=True),
        lax.psum_scatter(fc2_grad, "dp", scatter_dimension=1, tiled=True),
        lax.psum_scatter(flattened, "dp", scatter_dimension=0, tiled=True),
    )
    summed = unpack_vectors(lax.all_gather(flat_sum, "dp", axis=0, tiled=True), vectors)
    return (
        block_out,
        tokens_grad,
        qkv_sum,
        summed[0],
        out_sum,
        summed[1],
        fc1_sum,
        summed[2],
        fc2_sum,
        summed[3],
        summed[4],
        summed[5],
        summed[6],
        summed[7],
    )


MESH = pl.DeviceIdType.MESH
BF16 = jnp.bfloat16
F32 = jnp.float32
GROUP = 4
SLOT = 256


def plain(left, right):
    return jnp.dot(left, right, preferred_element_type=F32)


def column_sum(values):
    return jnp.sum(values, axis=0, keepdims=True)


def layer_kernel(
    tokens, cotangent, lengths, ln1_gain, ln1_bias, qkv_weight, qv_bias, out_weight, out_bias,
    ln2_gain, ln2_bias, fc1_weight, fc1_bias, fc2_weight, fc2_bias,
    block_out, tokens_grad, fc1_out, fc2_out, out_out, qkv_out, vector_out,
    norm_one, inverse_one, normed, query, keys, values, probs, attn, weights_all,
    middle, norm_two, inverse_two, normed_two, hidden, grad_pre, grad_y,
    part_two, from_two, part_y, from_y, branch, grad_middle, grad_attn,
    key_sum, value_sum, stacked, part_one, from_one,
    own, from_x, summed, from_z, vector, vec_t, vec_x, vec_z,
    e0_send, e0_recv, e1_send, e1_recv, e2_send, e2_recv, e3_send, e3_recv,
    e4_send, e4_recv, e5_send, e5_recv, x_send, x_recv, z_send, z_recv,
    vt_send, vt_recv, vx_send, vx_recv, vz_send, vz_recv,
):
    share = tokens.shape[0] // GROUP
    width = qkv_weight.shape[1]
    heads = width // HEAD_DIM
    scale = HEAD_DIM ** (-0.5)
    steps = own[0].shape[0]
    t = lax.axis_index("tensor")
    d = lax.axis_index("dp")
    z, x = d // 2, d % 2
    other = d + 1 - 2 * x
    core = t + 1 - 2 * lax.rem(t, 2)
    across = lax.rem(t + 2, GROUP)
    cross = lax.rem(core + 2, GROUP)
    peers = (core, across)
    order = (cross, across, core, t)
    zs = [lax.rem(z + s, steps) for s in range(1, steps)]

    barrier = pltpu.get_barrier_semaphore()
    for peer in peers:
        pl.semaphore_signal(barrier, inc=1, device_id={"tensor": peer}, device_id_type=MESH)
    pl.semaphore_signal(barrier, inc=1, device_id={"dp": other}, device_id_type=MESH)
    for to in zs:
        pl.semaphore_signal(barrier, inc=1, device_id={"dp": 2 * to + x}, device_id_type=MESH)
    pl.semaphore_wait(barrier, len(peers) + 1 + len(zs))

    def remote(src, dst, send, recv, **target):
        return pltpu.make_async_remote_copy(
            src_ref=src, dst_ref=dst, send_sem=send, recv_sem=recv,
            device_id=target, device_id_type=MESH,
        )

    pending = []

    def begin(copy):
        copy.start()
        pending.append(copy)

    def rows(i):
        return pl.ds(share * i, share)

    def rows_of(i):
        return pl.ds(pl.multiple_of(share * i, share), share)

    def block_copy(ref, at, send, recv, s):
        view = ref.at[at]
        return remote(view, view, send.at[s], recv.at[s], tensor=(core, across, core)[s])

    def spread(ref, at, send, recv):
        begin(block_copy(ref, at(t), send, recv, 0))
        begin(block_copy(ref, at(t), send, recv, 1))

    def forward(ref, at, send, recv):
        block_copy(ref, at(across), send, recv, 1).wait_recv()
        begin(block_copy(ref, at(across), send, recv, 2))

    def arrive(ref, at, send, recv):
        block_copy(ref, at(core), send, recv, 0).wait_recv()
        block_copy(ref, at(cross), send, recv, 2).wait_recv()

    weights_all[t] = out_weight[...]
    whole = lambda u: u
    spread(weights_all, whole, e0_send, e0_recv)
    gains = [ref[...].reshape(1, -1) for ref in (ln1_gain, ln1_bias, out_bias, ln2_gain, ln2_bias, fc1_bias, fc2_bias)]
    gain_one, bias_one, bias_out, gain_two, bias_two, bias_fc1, bias_fc2 = gains

    length = lengths[0, 0]
    column = lax.broadcasted_iota(jnp.int32, (1, width), 1) // HEAD_DIM
    picks = [(column == h).astype(BF16) for h in range(heads)]
    vector[...] = jnp.zeros_like(vector)

    for i in range(GROUP):
        n, inverse = normalize(tokens[rows(i), :].astype(F32))
        norm_one[rows(i), :] = n
        inverse_one[rows(i), :] = inverse
        low = (n * gain_one + bias_one).astype(BF16)
        normed[rows(i), :] = low
        query[rows(i), :] = (right_product(low, qkv_weight[0]) + qv_bias[0:1, :]).astype(BF16)
        keys[rows(i), :] = right_product(low, qkv_weight[1]).astype(BF16)
        values[rows(i), :] = (right_product(low, qkv_weight[2]) + qv_bias[1:2, :]).astype(BF16)
        live = lax.broadcasted_iota(jnp.int32, (share, 1), 0) + share * i < length
        g = cotangent[rows(i), :].astype(F32) * live.astype(F32)
        grad_y[rows(i), :] = g.astype(BF16)
        vector[9:10, :] += column_sum(g)

    def tile(i):
        return lambda u: (u, rows(i))

    for i in range(GROUP):
        span = share * (i + 1)
        row = lax.broadcasted_iota(jnp.int32, (share, span), 0) + share * i
        col = lax.broadcasted_iota(jnp.int32, (share, span), 1)
        allowed = ((col <= row) & (row < length)) | (col == row)
        mixed = jnp.zeros((share, width), F32)
        k, v = keys[0:span, :], values[0:span, :]
        for h in range(heads):
            scores = right_product(query[rows(i), :] * picks[h], k) * scale
            scores = jnp.where(allowed, scores, NEG)
            e = jnp.exp(scores - jnp.max(scores, axis=-1, keepdims=True))
            p = e / jnp.sum(e, axis=-1, keepdims=True)
            probs[h, rows(i), 0:span] = p
            mixed += plain(p.astype(BF16), v * picks[h])
        attn[t, rows(i), :] = mixed.astype(BF16)
        if i == 0:
            forward(weights_all, whole, e0_send, e0_recv)
        if i > 0:
            forward(attn, tile(i - 1), e1_send.at[i - 1], e1_recv.at[i - 1])
        spread(attn, tile(i), e1_send.at[i], e1_recv.at[i])
    forward(attn, tile(GROUP - 1), e1_send.at[GROUP - 1], e1_recv.at[GROUP - 1])
    arrive(weights_all, whole, e0_send, e0_recv)

    def send_share(step, value, part, landing, send, recv):
        if step == 1:
            share_copy(0, part, landing, send, recv).wait_recv()
            value = value + landing[0].astype(F32)
        part[step] = value.astype(BF16)
        if step < 3:
            begin(share_copy(step, part, landing, send, recv))

    def share_copy(step, part, landing, send, recv):
        return remote(
            part.at[step], landing.at[step], send.at[step], recv.at[step],
            tensor=(core, across, core)[step],
        )

    def sum_shares(part, landing, send, recv):
        for step in (1, 2):
            share_copy(step, part, landing, send, recv).wait_recv()
        return part[3].astype(F32) + landing[2].astype(F32) + landing[1].astype(F32)

    curve = (2.0 / jnp.pi) ** 0.5
    for i in range(GROUP):
        arrive(attn, tile(i), e1_send.at[i], e1_recv.at[i])
    for step, i in enumerate(order):
        mid = tokens[rows_of(i), :].astype(F32) + bias_out
        for u in range(GROUP):
            mid += plain(attn[u, rows_of(i), :], weights_all[u])
        middle[rows_of(i), :] = mid
        n, inverse = normalize(mid)
        norm_two[rows_of(i), :] = n
        inverse_two[rows_of(i), :] = inverse
        low = (n * gain_two + bias_two).astype(BF16)
        normed_two[rows_of(i), :] = low
        pre = plain(low, fc1_weight[...]) + bias_fc1
        square = pre * pre
        th = jnp.tanh(curve * (pre + 0.044715 * square * pre))
        half = 0.5 * (1.0 + th)
        hidden[rows_of(i), :] = (pre * half).astype(BF16)
        slope = half + 0.5 * pre * (1.0 - th * th) * (curve * (1.0 + 0.134145 * square))
        gp = (slope * right_product(grad_y[rows_of(i), :], fc2_weight[...])).astype(BF16)
        grad_pre[rows_of(i), :] = gp
        vector[10:11, :] += column_sum(gp.astype(F32))
        gn = right_product(gp, fc1_weight[...])
        vector[2:3, :] += column_sum(gn * n)
        vector[3:4, :] += column_sum(gn)
        send_share(step, gn, part_two, from_two, e2_send, e2_recv)

    def x_copy(p):
        return remote(own[p].at[:, 1 - x], from_x[p], x_send.at[p], x_recv.at[p], dp=other)

    def x_start(p, grad):
        own[p][...] = grad.astype(BF16).reshape(own[p].shape)
        x_copy(p).start()

    def z_copy(p, s):
        return remote(
            summed[p].at[zs[s]], from_z[p].at[s], z_send.at[p, s], z_recv.at[p, s],
            dp=2 * zs[s] + x,
        )

    def z_start(p):
        x_copy(p).wait()
        for k in range(steps):
            summed[p][k] = (own[p][k, x].astype(F32) + from_x[p][k].astype(F32)).astype(BF16)
        for s in range(steps - 1):
            z_copy(p, s).start()

    def z_finish(p):
        total = summed[p][z].astype(F32)
        for s in range(steps - 1):
            z_copy(p, s).wait()
            total += from_z[p][s].astype(F32)
        return total

    x_start(0, left_product(grad_y[...], hidden[...]))
    for step, i in enumerate(order):
        y = plain(hidden[rows_of(i), :], fc2_weight[...])
        send_share(step, y, part_y, from_y, e5_send, e5_recv)

    mine = rows_of(t)
    gn = sum_shares(part_two, from_two, e2_send, e2_recv)
    position = lax.broadcasted_iota(jnp.int32, (share, 1), 0) + share * t
    live = (position < length).astype(F32)
    gm = grad_y[mine, :].astype(F32) + norm_back(gn, norm_two[mine, :], inverse_two[mine, :], gain_two)
    grad_middle[...] = gm
    branch[t] = gm.astype(BF16)
    spread(branch, whole, e3_send, e3_recv)

    x_start(1, left_product(normed_two[...], grad_pre[...]))
    result = middle[mine, :] + sum_shares(part_y, from_y, e5_send, e5_recv) + bias_fc2
    block_out[...] = (live * result).astype(BF16)
    z_start(0)

    forward(branch, whole, e3_send, e3_recv)
    arrive(branch, whole, e3_send, e3_recv)
    for i in range(GROUP):
        grad_attn[rows(i), :] = right_product(branch[i], out_weight[...]).astype(BF16)
        vector[8:9, :] += column_sum(branch[i].astype(F32))
    x_start(2, left_product(branch[...].reshape(tokens.shape), attn[t]))

    key_sum[...] = jnp.zeros_like(key_sum)
    value_sum[...] = jnp.zeros_like(value_sum)
    for i in range(GROUP):
        span = share * (i + 1)
        k, v = keys[0:span, :], values[0:span, :]
        query_sum = jnp.zeros((share, width), F32)
        for h in range(heads):
            p = probs[h, rows(i), 0:span]
            ga = grad_attn[rows(i), :] * picks[h]
            gprob = right_product(ga, v)
            centre = jnp.sum(p * gprob, axis=-1, keepdims=True)
            gs = (p * (gprob - centre)).astype(BF16)
            query_sum += plain(gs, k * picks[h])
            key_sum[0:span, :] += left_product(gs, query[rows(i), :] * picks[h])
            value_sum[0:span, :] += left_product(p.astype(BF16), ga)
        stacked[rows(i), 0:width] = (query_sum * scale).astype(BF16)
        if i == 1:
            z_start(1)
    stacked[:, SLOT : SLOT + width] = (key_sum[...] * scale).astype(BF16)
    stacked[:, 2 * SLOT : 2 * SLOT + width] = value_sum[...].astype(BF16)
    for j in range(3):
        x_start(3 + j, left_product(normed[...], stacked[:, SLOT * j : SLOT * j + width]))

    vector[11:12, 0:width] = column_sum(stacked[:, 0:width].astype(F32))
    vector[12:13, 0:width] = column_sum(stacked[:, 2 * SLOT : 2 * SLOT + width].astype(F32))
    for step, i in enumerate(order):
        gn = jnp.zeros((share, tokens.shape[1]), F32)
        for j in range(3):
            gn += plain(stacked[rows_of(i), SLOT * j : SLOT * j + width], qkv_weight[j])
        vector[0:1, :] += column_sum(gn * norm_one[rows_of(i), :])
        vector[1:2, :] += column_sum(gn)
        send_share(step, gn, part_one, from_one, e4_send, e4_recv)

    vec_t[t] = vector[0:8, :]
    spread(vec_t, whole, vt_send, vt_recv)
    z_start(2)
    forward(vec_t, whole, vt_send, vt_recv)
    arrive(vec_t, whole, vt_send, vt_recv)
    vector[0:8, :] = vec_t[0] + vec_t[1] + vec_t[2] + vec_t[3]
    pair = remote(vector, vec_x, vx_send, vx_recv, dp=other)
    pair.start()
    for j in range(3):
        z_start(3 + j)
    pair.wait()
    vec_z[z] = vector[...] + vec_x[...]
    for s, to in enumerate(zs):
        begin(remote(vec_z.at[z], vec_z.at[z], vz_send.at[s], vz_recv.at[z], dp=2 * to + x))

    gn = sum_shares(part_one, from_one, e4_send, e4_recv)
    tokens_grad[...] = grad_middle[...] + norm_back(
        gn, norm_one[mine, :], inverse_one[mine, :], gain_one
    )
    fc2_out[...] = z_finish(0)
    fc1_out[...] = z_finish(1)
    out_out[...] = z_finish(2)
    for j in range(3):
        qkv_out[j] = z_finish(3 + j)
    for s, to in enumerate(zs):
        remote(vec_z.at[to], vec_z.at[to], vz_send.at[s], vz_recv.at[to], dp=2 * to + x).wait_recv()
    total = vec_z[0]
    for k in range(1, steps):
        total += vec_z[k]
    vector_out[...] = total
    for copy in pending:
        copy.wait_send()


def place_kernel(
    block, grad, qkv, out, fc1, fc2, vec,
    block_to, grad_to, qkv_to, qv_to, out_to, out_bias_to, fc1_to, fc1_bias_to, fc2_to, fc2_bias_to,
    *norm_to,
):
    pairs = ((block, block_to), (grad, grad_to), (qkv, qkv_to), (out, out_to), (fc1, fc1_to), (fc2, fc2_to))
    for source, target in pairs:
        target[...] = source[...]
    qv_to[...] = vec[11:13, 0 : qv_to.shape[1]]
    lines = ((8, out_bias_to), (10, fc1_bias_to), (9, fc2_bias_to), *enumerate(norm_to))
    for row, target in lines:
        target[...] = vec[row, :]


def fused(
    tokens, cotangent, seq_lengths, ln1_gain, ln1_bias, qkv_weight, qv_bias, out_weight, out_bias,
    ln2_gain, ln2_bias, fc1_weight, fc1_bias, fc2_weight, fc2_bias,
):
    count, depth = tokens.shape
    width = qkv_weight.shape[2]
    units = fc1_weight.shape[1]
    heads = width // HEAD_DIM
    share = count // GROUP
    members = lax.axis_size("dp")
    steps = members // 2
    chunk = depth // members
    widths = (units, units, width, width, width, width)
    vmem = pltpu.VMEM
    dma = pltpu.SemaphoreType.DMA
    parts = len(widths)
    scratch = [
        vmem((count, depth), F32), vmem((count, 1), F32), vmem((count, depth), BF16),
        vmem((count, width), BF16), vmem((count, width), BF16), vmem((count, width), BF16),
        vmem((heads, count, count), F32),
        vmem((GROUP, count, width), BF16), vmem((GROUP, width, depth), BF16),
        vmem((count, depth), F32), vmem((count, depth), F32), vmem((count, 1), F32),
        vmem((count, depth), BF16), vmem((count, units), BF16), vmem((count, units), BF16),
        vmem((count, depth), BF16),
        vmem((GROUP, share, depth), BF16), vmem((GROUP, share, depth), BF16),
        vmem((GROUP, share, depth), BF16), vmem((GROUP, share, depth), BF16),
        vmem((GROUP, share, depth), BF16), vmem((share, depth), F32), vmem((count, width), BF16),
        vmem((count, width), F32), vmem((count, width), F32), vmem((count, 3 * SLOT), BF16),
        vmem((GROUP, share, depth), BF16), vmem((GROUP, share, depth), BF16),
        [vmem((steps, 2, chunk, w), BF16) for w in widths],
        [vmem((steps, chunk, w), BF16) for w in widths],
        [vmem((steps, chunk, w), BF16) for w in widths],
        [vmem((steps - 1, chunk, w), BF16) for w in widths],
        vmem((16, depth), F32), vmem((GROUP, 8, depth), F32), vmem((16, depth), F32),
        vmem((steps, 16, depth), F32),
        dma((3,)), dma((3,)),
        dma((GROUP, 3)), dma((GROUP, 3)),
        dma((3,)), dma((3,)),
        dma((3,)), dma((3,)),
        dma((3,)), dma((3,)),
        dma((3,)), dma((3,)),
        dma((parts,)), dma((parts,)),
        dma((parts, steps - 1)), dma((parts, steps - 1)),
        dma((3,)), dma((3,)),
        dma, dma,
        dma((steps - 1,)), dma((steps,)),
    ]
    in_vmem = pl.BlockSpec(memory_space=pltpu.VMEM)
    shape = jax.ShapeDtypeStruct
    block, grad, fc1, fc2, out, qkv, vec = pl.pallas_call(
        layer_kernel,
        out_shape=(
            shape((share, depth), BF16), shape((share, depth), F32), shape((chunk, units), F32),
            shape((chunk, units), F32), shape((chunk, width), F32), shape((3, chunk, width), F32),
            shape((16, depth), F32),
        ),
        in_specs=[in_vmem] * 2 + [pl.BlockSpec(memory_space=pltpu.SMEM)] + [in_vmem] * 12,
        out_specs=(in_vmem,) * 7,
        scratch_shapes=scratch,
        compiler_params=pltpu.CompilerParams(
            collective_id=0, has_side_effects=True, vmem_limit_bytes=56 * 2**20
        ),
        name="layer",
    )(
        tokens, cotangent, seq_lengths, ln1_gain, ln1_bias, qkv_weight.transpose(0, 2, 1), qv_bias,
        out_weight, out_bias, ln2_gain, ln2_bias, fc1_weight, fc1_bias, fc2_weight, fc2_bias,
    )
    line = shape((depth,), F32)
    block, grad, qkv, qv, out, lined_out, fc1, lined_fc1, fc2, lined_fc2, *norms = pl.pallas_call(
        place_kernel,
        out_shape=(
            shape(block.shape, BF16), shape(grad.shape, F32), shape(qkv.shape, F32),
            shape((2, width), F32), shape(out.shape, F32), line, shape(fc1.shape, F32), line,
            shape(fc2.shape, F32), line, line, line, line, line,
        ),
        in_specs=[in_vmem] * 7,
        out_specs=(in_vmem,) * 14,
        name="place",
    )(block, grad, qkv, out, fc1, fc2, vec)
    return (block, grad, qkv, qv, out.T, lined_out, fc1, lined_fc1, fc2.T, lined_fc2, *norms)


def layer(*arguments):
    count, depth = arguments[0].shape
    members = lax.axis_size("dp")
    fits = (
        lax.axis_size("tensor") == GROUP
        and count == MAXLEN
        and arguments[2].shape[1] == 1
        and members % 2 == 0
        and depth % (16 * members) == 0
        and arguments[11].shape[1] == depth
    )
    return fused(*arguments) if fits else shards(*arguments)


def solution(mesh):
    placed = (
        P("dp", None),
        P("dp", None),
        P("dp", None),
        P(),
        P(),
        P(None, None, "tensor"),
        P(None, "tensor"),
        P("tensor", None),
        P(),
        P(),
        P(),
        P(None, "tensor"),
        P("tensor"),
        P("tensor", None),
        P(),
    )
    return jax.shard_map(
        layer,
        mesh=mesh,
        in_specs=placed,
        out_specs=(
            P(("dp", "tensor"), None),
            P(("dp", "tensor"), None),
            P(None, "dp", "tensor"),
            P(None, "tensor"),
            P("tensor", "dp"),
            P(),
            P("dp", "tensor"),
            P("tensor"),
            P("tensor", "dp"),
            P(),
            P(),
            P(),
            P(),
            P(),
        ),
        check_vma=False,
    )
```
